32 devices in a mesh: row: 4 (over x, core), loop: 8 (over z, y).
Axes of the slice: x: 2, y: 2, z: 4, core: 2. Of those that a mesh axis runs over, the one named last changes fastest.
Arguments:
- amplitudes: float32 [8192, 6144], P('row', 'loop'), may hold values from -6 to 6
- integrals: float32 [8192, 2048], P('row', 'loop'), may hold values from -0.09375 to 0.09375
- screen_mask: int32 [64, 16], P('row'), may hold values 0 or 1
- base_residual: float32 [2048, 6144], P('row', 'loop'), may hold values from -6 to 6
- vir_energy: float32 [2048], P('row'), may hold values from 0.5 to 4
- occ_energy: float32 [6144], P('loop'), may hold values from 0.5 to 2
Outputs:
- residual: float32 [2048, 6144], P('row', 'loop')
- update: float32 [2048, 6144], P('row', 'loop')
The draws below stay inside these ranges and needn't reach their ends.
All inputs are finite; a program needn't handle non-finite values. No bound on the sum of `screen_mask` on one device may be relied on, other than what follows from the above.
Results may differ from the reference program's by a relative error of at most 0.000068.
Values sent between devices are 32-bit elements; how exact they have to be, the bound alone decides.
No kernel may reach another device: no remote copies, remote signals or barrier semaphores. Data moves between devices by JAX's collectives and lax.ppermute only.
A program may use at most 128 MiB of HBM per device.

```python
import math
import jax
import jax.numpy as jnp
from jax import lax

TILE = 128
AB = 2048
CD = 8192
IJ = 6144


def with_ends(result, rng, low, largest):
    shape = result.shape
    index_at = [jax.random.randint(jax.random.fold_in(rng, axis), (), 0, shape[axis]) for axis in range(len(shape))]
    result = result.at[tuple(index_at)].set(low)
    longest = shape.index(max(shape))
    index_at[longest] = (index_at[longest] + 1) % shape[longest]
    return result.at[tuple(index_at)].set(largest)


def level_of(own_key, dims, cuts, least, high):
    gain = 1.0
    for position, blocks in cuts:
        draws = jax.random.uniform(jax.random.fold_in(jax.random.fold_in(own_key, 6), position), (blocks,), jnp.float32, least / len(cuts), high / len(cuts))
        gain = gain * jnp.repeat(jnp.exp(draws), dims[position] // blocks).reshape((-1,) + (1,) * (len(dims) - 1 - position))
    return gain


def bell_draw(own_key, dims, deviation, reach, pieces=(), dtype=jnp.bfloat16):
    gain = level_of(own_key, dims, pieces, -0.22, 0.18) if pieces else 1.0
    result = jax.random.normal(own_key, dims, jnp.float32) * deviation * gain
    return jnp.minimum(jnp.maximum(result, -reach), reach).astype(dtype)


def setup_inputs(seed: int = 0) -> dict:
    arg_keys = jax.random.split(jax.random.key(seed), 7)
    amplitudes = bell_draw(arg_keys[0], (CD, IJ), 1.0, 6.0, ((0, 4), (1, 8)), jnp.float32)
    integrals = bell_draw(arg_keys[1], (CD, AB), (CD // 2) ** -0.5, 0.09375, ((0, 4), (1, 8)), jnp.float32)
    screen_mask = with_ends((jax.random.randint(arg_keys[2], (CD // TILE, AB // TILE), 0, 2) < 1).astype(jnp.int32), jax.random.fold_in(arg_keys[2], 1), 0, 1)
    base_residual = bell_draw(arg_keys[3], (AB, IJ), 1.0, 6.0, ((0, 4), (1, 8)), jnp.float32)
    vir_energy = jnp.clip(jnp.exp(math.log(4.0) - 2.0794415 * jax.random.uniform(arg_keys[4], (AB,), jnp.float32) ** level_of(arg_keys[4], (AB,), ((0, 4),), -0.2, 0.2)), 0.5, 4.0)
    occ_energy = jnp.clip(jnp.exp(math.log(2.0) - 1.3862944 * jax.random.uniform(arg_keys[5], (IJ,), jnp.float32) ** level_of(arg_keys[5], (IJ,), ((0, 8),), -0.2, 0.2)), 0.5, 2.0)
    return {"amplitudes": amplitudes, "integrals": integrals, "screen_mask": screen_mask, "base_residual": base_residual, "vir_energy": vir_energy, "occ_energy": occ_energy}


def expand_mask(screen_mask, tile):
    rows_t, cols_t = screen_mask.shape
    values = screen_mask.astype(jnp.float32)
    return jnp.broadcast_to(values[:, None, :, None], (rows_t, tile, cols_t, tile)).reshape(rows_t * tile, cols_t * tile)


def reference(amplitudes, integrals, screen_mask, base_residual, vir_energy, occ_energy):
    screened = integrals * expand_mask(screen_mask, TILE)
    ladder = lax.dot_general(screened, amplitudes, (((0,), (0,)), ((), ())), precision=lax.Precision.HIGHEST, preferred_element_type=jnp.float32)
    residual = base_residual + ladder
    update = residual / (vir_energy[:, None] + occ_energy[None, :])
    return residual, update
```

```python
import functools

import jax
import jax.numpy as jnp
from jax import lax
from jax.experimental import pallas as pl
from jax.experimental.pallas import tpu as pltpu
from jax.sharding import PartitionSpec as P

TILE = 128
GROUP = 8
HEAD = 16
VMEM_LIMIT = 48 * 1024 * 1024
PLANS = ((24, 8), (28, 10), (32, 14), (32, 32))

ANY = pl.BlockSpec(memory_space=pl.ANY)
SMEM = pl.BlockSpec(memory_space=pltpu.SMEM)
VMEM = pl.BlockSpec(memory_space=pltpu.VMEM)


def expand_mask(screen_mask, tile):
    rows_t, cols_t = screen_mask.shape
    values = screen_mask.astype(jnp.float32)
    return jnp.broadcast_to(values[:, None, :, None], (rows_t, tile, cols_t, tile)).reshape(
        rows_t * tile, cols_t * tile
    )


def gathered(amplitudes, integrals, screen_mask, base_residual, vir_energy, occ_energy):
    full_mask = expand_mask(screen_mask, TILE)
    assembled = lax.all_gather(integrals, "loop", axis=1, tiled=True)
    partial = lax.dot_general(
        assembled * full_mask,
        amplitudes,
        (((0,), (0,)), ((), ())),
        precision=lax.Precision.HIGHEST,
        preferred_element_type=jnp.float32,
    )
    ladder = lax.psum_scatter(partial, "row", scatter_dimension=0, tiled=True)
    residual = base_residual + ladder
    return residual, residual / (vir_energy[:, None] + occ_energy[None, :])


def kept_in_block(mask_ref, block):
    rows = mask_ref.shape[0]

    def add(i, total):
        return total + mask_ref[i, 2 * block] + mask_ref[i, 2 * block + 1]

    return lax.fori_loop(0, rows, add, jnp.int32(0))


def pack_kernel(place_ref, mask_ref, integrals_ref, *out_refs):
    block = place_ref[0]
    rank = jnp.int32(0)
    for jj in range(2):

        def step(i, rank, jj=jj):
            kept = mask_ref[i, 2 * block + jj]
            row = pl.ds(pl.multiple_of(i * TILE, TILE), TILE)
            for part, out_ref in enumerate(out_refs):

                @pl.when((kept == 1) & (rank >= part * GROUP) & (rank < (part + 1) * GROUP))
                def _():
                    out_ref[rank - part * GROUP] = integrals_ref[row, pl.ds(jj * TILE, TILE)]

            return rank + kept

        rank = lax.fori_loop(0, mask_ref.shape[0], step, rank)


def pack(place, mask, integrals):
    shape = jax.ShapeDtypeStruct((GROUP, TILE, TILE), jnp.float32)
    parts = 2 * mask.shape[0] // GROUP
    return pl.pallas_call(
        pack_kernel,
        out_shape=[shape] * parts,
        in_specs=[SMEM, SMEM, VMEM],
        out_specs=[VMEM] * parts,
        compiler_params=pltpu.CompilerParams(vmem_limit_bytes=VMEM_LIMIT),
        cost_estimate=pl.CostEstimate(flops=0, bytes_accessed=4 << 20, transcendentals=0),
        name="pack",
    )(place, mask, integrals)


def rest_kernel(place_ref, mask_ref, mine_ref, other_ref, out_ref):
    slots = out_ref.shape[0]
    mine = jnp.maximum(kept_in_block(mask_ref, place_ref[0]) - HEAD, 0)
    other = jnp.maximum(kept_in_block(mask_ref, place_ref[1]) - HEAD, 0)

    def put_mine(k, carry):
        out_ref[jnp.minimum(k, slots - 1)] = mine_ref[k]
        return carry

    def put_other(k, carry):
        out_ref[jnp.minimum(mine + k, slots - 1)] = other_ref[k]
        return carry

    lax.fori_loop(0, jnp.minimum(mine, mine_ref.shape[0]), put_mine, 0)
    lax.fori_loop(0, jnp.minimum(other, other_ref.shape[0]), put_other, 0)


def rest(place, mask, mine, other, slots):
    return pl.pallas_call(
        rest_kernel,
        out_shape=jax.ShapeDtypeStruct((slots, TILE, TILE), jnp.float32),
        in_specs=[SMEM, SMEM, VMEM, VMEM],
        out_specs=VMEM,
        compiler_params=pltpu.CompilerParams(vmem_limit_bytes=VMEM_LIMIT),
        cost_estimate=pl.CostEstimate(flops=0, bytes_accessed=2 << 20, transcendentals=0),
        name="rest",
    )(place, mask, mine, other)


def split(x):
    high = x.astype(jnp.bfloat16)
    return high, (x - high.astype(jnp.float32)).astype(jnp.bfloat16)


def split_kernel(x_ref, high_ref, low_ref):
    high_ref[...], low_ref[...] = split(x_ref[...])


def split_array(x):
    rows, cols = x.shape
    step = rows // 8
    spec = pl.BlockSpec((step, cols), lambda i: (i, 0))
    shape = jax.ShapeDtypeStruct(x.shape, jnp.bfloat16)
    return pl.pallas_call(
        split_kernel,
        grid=(rows // step,),
        out_shape=[shape, shape],
        in_specs=[spec],
        out_specs=[spec, spec],
        compiler_params=pltpu.CompilerParams(vmem_limit_bytes=VMEM_LIMIT),
        cost_estimate=pl.CostEstimate(flops=3 * x.size, bytes_accessed=8 * x.size, transcendentals=0),
        name="split",
    )(x)


def stage_kernel(layout, shared, place_ref, mask_ref, high_ref, low_ref, *refs):
    n_tiles = len(layout)
    tile_refs, refs = refs[:n_tiles], refs[n_tiles:]
    keep_ref, send_ref, mine, other, sem, i_high, i_low = refs
    slots = (mine, other)
    core = place_ref[2]

    @pl.when(pl.program_id(0) == 0)
    def _():
        copies = []
        for ref, targets in zip(tile_refs, layout):
            for which, start in targets:
                copy = pltpu.make_async_copy(
                    ref, slots[which].at[pl.ds(start, ref.shape[0])], sem.at[len(copies)]
                )
                copy.start()
                copies.append(copy)
        for copy in copies:
            copy.wait()
        extra = jnp.int32(0)
        for which in range(2):
            block = place_ref[which]
            rank = jnp.int32(0)
            for jj in range(2):
                row = jnp.where(core == jj, 0, 2 * TILE) + which * TILE
                row = pl.ds(pl.multiple_of(row, TILE), TILE)

                def step(i, rank, which=which, jj=jj, block=block, row=row, extra=extra):
                    kept = mask_ref[i, 2 * block + jj]
                    column = pl.ds(pl.multiple_of(i * TILE, TILE), TILE)

                    @pl.when(kept == 1)
                    def _():
                        slot = jnp.where(rank < HEAD, rank, rank + extra)
                        slot = jnp.minimum(slot, slots[which].shape[0] - 1)
                        high, low = split(jnp.swapaxes(slots[which][slot], 0, 1))
                        i_high[row, column] = high
                        i_low[row, column] = low

                    @pl.when(kept != 1)
                    def _():
                        i_high[row, column] = jnp.zeros((TILE, TILE), jnp.bfloat16)
                        i_low[row, column] = jnp.zeros((TILE, TILE), jnp.bfloat16)

                    return rank + kept

                rank = lax.fori_loop(0, mask_ref.shape[0], step, rank)
            if shared:
                extra = jnp.maximum(rank - HEAD, 0)

    def dot(a, b):
        return jnp.dot(a, b, preferred_element_type=jnp.float32)

    total = dot(i_low[...], high_ref[...]) + dot(i_high[...], low_ref[...])
    total = total + dot(i_high[...], high_ref[...])
    keep_ref[...] = total[: 2 * TILE]
    send_ref[...] = total[2 * TILE :]


def stage(place, mask, high, low, mine, other, shared):
    depth, width = high.shape
    step = 256
    tiles, layout = [], []
    ends = []
    for which, parts in enumerate((mine, other)):
        start = 0
        for part in parts:
            tiles.append(part)
            layout.append(((which, start),))
            start += part.shape[0]
        ends.append(start)
    if shared is not None:
        tiles.append(shared)
        layout.append(((0, ends[0]), (1, ends[1])))
        ends = [end + shared.shape[0] for end in ends]
    half = jax.ShapeDtypeStruct((2 * TILE, width), jnp.float32)
    column = pl.BlockSpec((depth, step), lambda n: (0, n))
    result = pl.BlockSpec((2 * TILE, step), lambda n: (0, n))
    return pl.pallas_call(
        functools.partial(stage_kernel, tuple(layout), shared is not None),
        grid=(width // step,),
        out_shape=[half, half],
        in_specs=[SMEM, SMEM, column, column] + [ANY] * len(tiles),
        out_specs=[result, result],
        scratch_shapes=[
            pltpu.VMEM((ends[0], TILE, TILE), jnp.float32),
            pltpu.VMEM((ends[1], TILE, TILE), jnp.float32),
            pltpu.SemaphoreType.DMA((sum(len(t) for t in layout),)),
            pltpu.VMEM((4 * TILE, depth), jnp.bfloat16),
            pltpu.VMEM((4 * TILE, depth), jnp.bfloat16),
        ],
        compiler_params=pltpu.CompilerParams(vmem_limit_bytes=VMEM_LIMIT),
        cost_estimate=pl.CostEstimate(
            flops=6 * 4 * TILE * depth * width, bytes_accessed=12 << 20, transcendentals=0
        ),
        name="stage",
    )(place, mask, high, low, *tiles)


def finish_kernel(n_stages, place_ref, base_ref, vir_ref, occ_ref, *refs):
    pieces, refs = refs[: 4 * n_stages], refs[4 * n_stages :]
    residual_ref, update_ref, held, sem = refs
    core, y, turn = place_ref[0], place_ref[1], place_ref[2]
    for s in range(n_stages):

        @pl.when(turn == s)
        def _():
            for k in range(4):
                pltpu.make_async_copy(pieces[4 * s + k], held.at[k], sem.at[k]).start()

    for k in range(4):
        pltpu.make_async_copy(pieces[k], held.at[k], sem.at[k]).wait()
    for half in range(2):
        for which in range(2):
            block = y if which == 0 else 1 - y
            tile = core if half == 0 else 1 - core
            rows = pl.ds(pl.multiple_of(block * 2 * TILE + tile * TILE, TILE), TILE)
            part = pl.ds(which * TILE, TILE)
            ladder = held[2 * half, part] + held[2 * half + 1, part]
            residual = base_ref[rows] + ladder
            residual_ref[rows] = residual
            update_ref[rows] = residual / (vir_ref[rows] + occ_ref[...])


def finish(place, base, vir, occ, pieces):
    shape = jax.ShapeDtypeStruct(base.shape, jnp.float32)
    n_stages = len(pieces)
    flat = [piece for stage_pieces in pieces for piece in stage_pieces]
    return pl.pallas_call(
        functools.partial(finish_kernel, n_stages),
        out_shape=[shape, shape],
        in_specs=[SMEM, VMEM, VMEM, VMEM] + [ANY] * len(flat),
        out_specs=[VMEM, VMEM],
        scratch_shapes=[
            pltpu.VMEM((4,) + flat[0].shape, jnp.float32),
            pltpu.SemaphoreType.DMA((4,)),
        ],
        compiler_params=pltpu.CompilerParams(vmem_limit_bytes=VMEM_LIMIT),
        cost_estimate=pl.CostEstimate(flops=4 * base.size, bytes_accessed=20 * base.size, transcendentals=0),
        name="finish",
    )(place, base, vir[:, None], occ[None, :], *flat)


def planned(amplitudes, integrals, screen_mask, base_residual, vir_energy, occ_energy):
    both = ("row", "loop")
    zs = range(4)
    row, loop = lax.axis_index("row"), lax.axis_index("loop")
    core, z, y = row % 2, loop // 2, loop % 2

    def around(x):
        return lax.ppermute(x, "loop", [(2 * a + b, 2 * ((a + 1) % 4) + b) for a in zs for b in range(2)])

    def across(x):
        return lax.ppermute(x, "loop", [(a, a ^ 1) for a in range(8)])

    def cores(x):
        return lax.ppermute(x, "row", [(0, 1), (1, 0), (2, 3), (3, 2)])

    def chips(x):
        return lax.ppermute(x, "row", [(0, 2), (2, 0), (1, 3), (3, 1)])

    def to_owner(x, s, flip):
        pairs = [
            ((((a - s) % 4) ^ flip) * 8 + 2 * a + b, ((a - s) % 4) * 8 + 2 * a + b) for a in zs for b in range(2)
        ]
        return lax.ppermute(x, both, pairs)

    def place_of(s):
        pair = 2 * ((z - s) % 4)
        return jnp.stack([pair + y, pair + 1 - y, core]).astype(jnp.int32)

    rows_t, cols_t = screen_mask.shape
    counts = screen_mask.reshape(rows_t, 8, cols_t // 8).sum((0, 2))
    most = counts.max()
    rests = jnp.maximum(counts - HEAD, 0).reshape(4, 2).sum(1).max()
    level = sum(((most > block) | (rests > more)).astype(jnp.float32) for block, more in PLANS[:-1])
    level = jnp.broadcast_to(level, (8, 128))
    level = jnp.maximum(level, cores(level))
    level = jnp.maximum(level, chips(level))[0, 0].astype(jnp.int32)

    parts = pack(place_of(0), screen_mask, integrals)
    first = (around(parts[0]), across(parts[0]))
    high, low = split_array(amplitudes)

    def run(block_limit, rest_limit, parts, first, high, low, mask):
        tails = parts[2:]
        tail_tiles = block_limit - HEAD
        tail = jnp.concatenate(tails)[:tail_tiles] if tail_tiles > GROUP else tails[0]
        other = [first[1], across(parts[1]), across(tail)]
        heads = [(first[0], around(parts[1]))]
        mixed = rest(place_of(0), mask, tail, other[2], rest_limit)
        heads.append(tuple(around(h) for h in heads[0]))
        rests = [around(mixed)]
        rests.append(around(rests[0]))
        heads.append(tuple(around(h) for h in heads[1]))
        rests.append(around(rests[1]))
        crossed = [tuple(across(h) for h in head) for head in heads]

        pieces = []
        for s in range(4):
            if s == 0:
                keep, send = stage(place_of(0), mask, high, low, list(parts), other, None)
            else:
                keep, send = stage(place_of(s), mask, high, low, heads[s - 1], crossed[s - 1], rests[s - 1])
            total = keep + cores(send)
            pieces.append((total, to_owner(total, s, 2), to_owner(total, s, 3), to_owner(total, s, 1)))
        return pieces

    pieces = lax.switch(
        level,
        [functools.partial(run, block, more) for block, more in PLANS],
        parts,
        first,
        high,
        low,
        screen_mask,
    )
    place = jnp.stack([core, y, (z - row) % 4]).astype(jnp.int32)
    return tuple(finish(place, base_residual, vir_energy, occ_energy, pieces))


def solution(mesh):
    in_specs = (
        P("row", "loop"),
        P("row", "loop"),
        P("row", None),
        P("row", "loop"),
        P("row"),
        P("loop"),
    )
    out_specs = (P("row", "loop"), P("row", "loop"))
    body = planned if (mesh.shape["row"], mesh.shape["loop"]) == (4, 8) else gathered
    return jax.shard_map(body, mesh=mesh, in_specs=in_specs, out_specs=out_specs, check_vma=False)
```

```python
import functools

import jax
import jax.numpy as jnp
from jax import lax
from jax.experimental import pallas as pl
from jax.experimental.pallas import tpu as pltpu
from jax.sharding import PartitionSpec as P

TILE = 128
GROUP = 8
HEAD = 16
VMEM_LIMIT = 16 * 1024 * 1024
UNIT = 4

COST = pl.CostEstimate(flops=1, bytes_accessed=1, transcendentals=0)
STAGE_COST = pl.CostEstimate(flops=40 * 1150 * 10**6, bytes_accessed=1, transcendentals=0)
ANY = pl.BlockSpec(memory_space=pl.ANY)
SMEM = pl.BlockSpec(memory_space=pltpu.SMEM)
VMEM = pl.BlockSpec(memory_space=pltpu.VMEM)
HBM = pl.BlockSpec(memory_space=pltpu.HBM)


def expand_mask(screen_mask, tile):
    rows_t, cols_t = screen_mask.shape
    values = screen_mask.astype(jnp.float32)
    return jnp.broadcast_to(values[:, None, :, None], (rows_t, tile, cols_t, tile)).reshape(
        rows_t * tile, cols_t * tile
    )


def gathered(amplitudes, integrals, screen_mask, base_residual, vir_energy, occ_energy):
    full_mask = expand_mask(screen_mask, TILE)
    assembled = lax.all_gather(integrals, "loop", axis=1, tiled=True)
    partial = lax.dot_general(
        assembled * full_mask,
        amplitudes,
        (((0,), (0,)), ((), ())),
        precision=lax.Precision.HIGHEST,
        preferred_element_type=jnp.float32,
    )
    ladder = lax.psum_scatter(partial, "row", scatter_dimension=0, tiled=True)
    residual = base_residual + ladder
    return residual, residual / (vir_energy[:, None] + occ_energy[None, :])


def kept_in_block(mask_ref, block):
    total = jnp.int32(0)
    for i in range(mask_ref.shape[0]):
        total = total + mask_ref[i, 2 * block] + mask_ref[i, 2 * block + 1]
    return total


def needs_kernel(mask_ref, out_ref):
    def step(pair, carry):
        more, units = carry
        rest = jnp.int32(0)
        for which in range(2):
            count = kept_in_block(mask_ref, 2 * pair + which)
            more = jnp.maximum(more, (count > HEAD + GROUP).astype(jnp.int32))
            rest = rest + jnp.maximum(count - HEAD, 0)
        units = jnp.maximum(units, (jnp.maximum(rest - GROUP, 0) + UNIT - 1) // UNIT)
        return more, units

    more, units = lax.fori_loop(0, mask_ref.shape[1] // 4, step, (jnp.int32(0), jnp.int32(0)))
    row = lax.broadcasted_iota(jnp.int32, out_ref.shape, 0)
    out_ref[...] = jnp.where(row == 0, more, units).astype(jnp.float32)


def needs(mask):
    return pl.pallas_call(
        needs_kernel,
        out_shape=jax.ShapeDtypeStruct((8, 128), jnp.float32),
        in_specs=[SMEM],
        out_specs=VMEM,
        cost_estimate=COST,
        name="needs",
    )(mask)


def pack_kernel(place_ref, mask_ref, integrals_ref, *out_refs):
    block = place_ref[0]
    rank = jnp.int32(0)
    for jj in range(2):

        def step(i, rank, jj=jj):
            kept = mask_ref[i, 2 * block + jj]
            row = pl.ds(pl.multiple_of(i * TILE, TILE), TILE)

            @pl.when(kept == 1)
            def _():
                tile = jnp.swapaxes(integrals_ref[row, pl.ds(jj * TILE, TILE)], 0, 1)
                head_ref, most_ref, last_ref = out_refs
                most = most_ref.shape[0]

                @pl.when(rank < HEAD)
                def _():
                    head_ref[rank] = tile

                @pl.when(rank < most)
                def _():
                    most_ref[rank] = tile

                @pl.when(rank >= most)
                def _():
                    last_ref[rank - most] = tile

            return rank + kept

        rank = lax.fori_loop(0, mask_ref.shape[0], step, rank)


def pack(place, mask, integrals):
    sizes = [HEAD, HEAD + GROUP, 2 * mask.shape[0] - HEAD - GROUP]
    shapes = [jax.ShapeDtypeStruct((size, TILE, TILE), jnp.float32) for size in sizes]
    return pl.pallas_call(
        pack_kernel,
        out_shape=shapes,
        in_specs=[SMEM, SMEM, VMEM],
        out_specs=[VMEM] * len(shapes),
        compiler_params=pltpu.CompilerParams(vmem_limit_bytes=VMEM_LIMIT),
        cost_estimate=COST,
        name="pack",
    )(place, mask, integrals)


def rest_kernel(n_mine, place_ref, first_ref, mask_ref, *refs):
    out_ref, held, sem = refs[-3:]
    first, slots = first_ref[0], out_ref.shape[0]
    start = -first
    blocks = (refs[:n_mine], refs[n_mine : 2 * n_mine])
    copies = []
    for which in range(2):
        to = 0
        for part, ref in enumerate(blocks[which]):
            skip = HEAD if part == 0 else 0
            size = ref.shape[0] - skip
            copy = pltpu.make_async_copy(
                ref.at[pl.ds(skip, size)], held.at[which, pl.ds(to, size)], sem.at[len(copies)]
            )
            copy.start()
            copies.append(copy)
            to += size
    for copy in copies:
        copy.wait()
    for which in range(2):
        count = jnp.maximum(kept_in_block(mask_ref, place_ref[which]) - HEAD, 0)
        for k in range(held.shape[1]):
            to = start + k

            @pl.when((k < count) & (to >= 0) & (to < slots))
            def _(k=k, to=to, which=which):
                out_ref[to] = held[which, k]

        start = start + count


def rest(place, first, mask, mine, other, slots, *earlier):
    size = sum(part.shape[0] for part in mine) - HEAD
    return pl.pallas_call(
        functools.partial(rest_kernel, len(mine)),
        out_shape=jax.ShapeDtypeStruct((slots, TILE, TILE), jnp.float32),
        in_specs=[SMEM] * 3 + [ANY] * (len(mine) + len(other) + len(earlier)),
        out_specs=VMEM,
        scratch_shapes=[
            pltpu.VMEM((2, size, TILE, TILE), jnp.float32),
            pltpu.SemaphoreType.DMA((2 * len(mine),)),
        ],
        compiler_params=pltpu.CompilerParams(vmem_limit_bytes=VMEM_LIMIT),
        cost_estimate=COST,
        name="rest",
    )(place, first, mask, *mine, *other, *earlier)


def room(shapes):
    return pl.pallas_call(
        lambda *refs: None,
        out_shape=[jax.ShapeDtypeStruct(shape, jnp.float32) for shape in shapes],
        out_specs=[ANY] * len(shapes),
        name="room",
    )()


def split(x):
    high = x.astype(jnp.bfloat16)
    return high, (x - high.astype(jnp.float32)).astype(jnp.bfloat16)


def split_kernel(x_ref, *refs):
    high_ref, low_ref, held, sem = refs[-4:]
    parts = held.shape[0]
    size = held.shape[1]
    copies = [
        pltpu.make_async_copy(x_ref.at[pl.ds(k * size, size)], held.at[k], sem.at[k]) for k in range(parts)
    ]
    for copy in copies:
        copy.start()
    for k in range(parts):
        copies[k].wait()
        rows = pl.ds(k * size, size)
        high_ref[rows], low_ref[rows] = split(held[k])


def split_array(x, *earlier):
    parts = 8
    shape = pltpu.VMEM(x.shape, jnp.bfloat16)
    return pl.pallas_call(
        split_kernel,
        out_shape=[shape, shape],
        in_specs=[ANY] * (1 + len(earlier)),
        out_specs=[VMEM, VMEM],
        scratch_shapes=[
            pltpu.VMEM((parts, x.shape[0] // parts, x.shape[1]), jnp.float32),
            pltpu.SemaphoreType.DMA((parts,)),
        ],
        compiler_params=pltpu.CompilerParams(vmem_limit_bytes=VMEM_LIMIT),
        cost_estimate=COST,
        name="split",
    )(x, *earlier)


def stage_kernel(sizes, place_ref, mask_ref, high_ref, low_ref, *refs):
    n_mine, n_other, n_rest = sizes
    mine_refs, refs = refs[:n_mine], refs[n_mine:]
    other_refs, refs = refs[:n_other], refs[n_other:]
    rest_refs = refs[:n_rest]
    keep_ref, send_ref, held, sem, i_low, i_high, out, out_sem = refs[-8:]
    rows_t = mask_ref.shape[0]
    stride = held.shape[0] // 2
    chunks, depth, width = i_low.shape[0], i_low.shape[2], high_ref.shape[1]
    step = 256
    core = place_ref[2]

    copies = []

    def bring(ref, start):
        copy = pltpu.make_async_copy(ref, held.at[pl.ds(start, ref.shape[0])], sem.at[len(copies)])
        copy.start()
        copies.append(copy)

    for which, block_refs in enumerate((mine_refs, other_refs)):
        start = which * stride
        for ref in block_refs:
            bring(ref, start)
            start += ref.shape[0]
        if n_rest:
            bring(rest_refs[0], start)
    ranks, totals = [], []
    for which in range(2):
        counts = []
        for jj in range(2):
            count = jnp.int32(0)
            for i in range(rows_t):
                count = count + mask_ref[i, 2 * place_ref[which] + jj]
            counts.append(count)
        ranks += [jnp.int32(0), counts[0]]
        totals.append(counts[0] + counts[1])
    extra = jnp.maximum(totals[0] - HEAD, 0) if n_rest else jnp.int32(0)
    for copy in copies:
        copy.wait()
    if n_rest:

        @pl.when(extra + jnp.maximum(totals[1] - HEAD, 0) > GROUP)
        def _():
            spilled = []
            for which in range(2):
                to = held.at[pl.ds(which * stride + HEAD + GROUP, rest_refs[1].shape[0])]
                spilled.append(pltpu.make_async_copy(rest_refs[1], to, sem.at[which]))
            for copy in spilled:
                copy.start()
            for copy in spilled:
                copy.wait()

    def unpack(k, ranks):
        ranks = list(ranks)
        for q in range(4):
            which, jj = q // 2, q % 2
            rows = pl.ds(q * TILE, TILE)
            for part in range(depth // TILE):
                kept = mask_ref[k * (depth // TILE) + part, 2 * place_ref[which] + jj]
                slot = jnp.where(ranks[q] < HEAD, ranks[q], ranks[q] + (extra if which else 0))
                slot = which * stride + jnp.minimum(slot, stride - 1)
                high, low = split(jnp.where(kept == 1, held[slot], 0.0))
                columns = pl.ds(part * TILE, TILE)
                i_high[k, rows, columns] = high
                i_low[k, rows, columns] = low
                ranks[q] = ranks[q] + kept
        return tuple(ranks)

    lax.fori_loop(0, chunks, unpack, tuple(ranks))

    def dot(a, b):
        return jnp.dot(a, b, preferred_element_type=jnp.float32)

    def out_copies(n):
        columns = pl.ds(pl.multiple_of(n * step, step), step)
        return [
            pltpu.make_async_copy(out.at[part, :, columns], ref.at[:, columns], out_sem.at[n, part])
            for part, ref in enumerate((keep_ref, send_ref))
        ]

    def product(n, carry):
        columns = pl.ds(pl.multiple_of(n * step, step), step)
        total = None
        for k in range(chunks):
            high = high_ref[pl.ds(k * depth, depth), columns]
            low = low_ref[pl.ds(k * depth, depth), columns]
            left = jnp.concatenate([i_low[k], i_high[k], i_high[k]], axis=1)
            part = dot(left, jnp.concatenate([high, low, high], axis=0))
            total = part if total is None else total + part
        first = jnp.concatenate([total[:TILE], total[2 * TILE : 3 * TILE]], axis=0)
        second = jnp.concatenate([total[TILE : 2 * TILE], total[3 * TILE :]], axis=0)
        out[0, :, columns] = jnp.where(core == 0, first, second)
        out[1, :, columns] = jnp.where(core == 0, second, first)
        for copy in out_copies(n):
            copy.start()
        return carry

    lax.fori_loop(0, width // step, product, 0)
    for n in range(width // step):
        for copy in out_copies(n):
            copy.wait()


def stage(place, mask, high, low, mine, other, rests, cost, earlier):
    rows, width = high.shape
    depth = 256
    half = pltpu.HBM((2 * TILE, width), jnp.float32)
    tiles = list(mine) + list(other) + list(rests)
    return pl.pallas_call(
        functools.partial(stage_kernel, (len(mine), len(other), len(rests))),
        out_shape=[half, half],
        in_specs=[SMEM, SMEM, VMEM, VMEM] + [HBM] * (len(tiles) + len(earlier)),
        out_specs=[ANY, ANY],
        scratch_shapes=[
            pltpu.VMEM((2 * (HEAD + 2 * mask.shape[0]), TILE, TILE), jnp.float32),
            pltpu.SemaphoreType.DMA((len(tiles) + 1,)),
            pltpu.VMEM((rows // depth, 4 * TILE, depth), jnp.bfloat16),
            pltpu.VMEM((rows // depth, 4 * TILE, depth), jnp.bfloat16),
            pltpu.VMEM((2, 2 * TILE, width), jnp.float32),
            pltpu.SemaphoreType.DMA((width // 256, 2)),
        ],
        compiler_params=pltpu.CompilerParams(vmem_limit_bytes=VMEM_LIMIT),
        cost_estimate=cost,
        name="stage",
    )(place, mask, *(pltpu.with_memory_space_constraint(a, pltpu.VMEM) for a in (high, low)), *tiles, *earlier)


def met(*arrays):
    return pl.pallas_call(
        lambda *refs: None,
        out_shape=jax.ShapeDtypeStruct((8, 128), jnp.float32),
        in_specs=[ANY] * len(arrays),
        out_specs=ANY,
        name="met",
    )(*arrays)


def add_kernel(a_ref, b_ref, *refs):
    refs[-1][...] = a_ref[...] + b_ref[...]


def add(a, b, *earlier):
    step = a.shape[0] // 2
    spec = pl.BlockSpec((step, a.shape[1]), lambda i: (i, 0))
    return pl.pallas_call(
        add_kernel,
        grid=(a.shape[0] // step,),
        out_shape=pltpu.HBM(a.shape, a.dtype),
        in_specs=[spec, spec] + [ANY] * len(earlier),
        out_specs=spec,
        compiler_params=pltpu.CompilerParams(vmem_limit_bytes=VMEM_LIMIT),
        cost_estimate=COST,
        name="add",
    )(a, b, *earlier)


def pass_kernel(turn_ref, *refs):
    pieces, (out_ref, held, sem) = refs[:-4], refs[-3:]
    for s in range(len(pieces) // 2):

        @pl.when(turn_ref[0] == s)
        def _():
            copies = [pltpu.make_async_copy(pieces[2 * s + k], held.at[k], sem.at[k]) for k in range(2)]
            for copy in copies:
                copy.start()
            for copy in copies:
                copy.wait()
            out_ref[...] = held[0] + held[1]


def to_pass(turn, pieces, later):
    shape = pieces[0][0].shape
    flat = [piece for pair in pieces for piece in pair]
    return pl.pallas_call(
        pass_kernel,
        out_shape=jax.ShapeDtypeStruct(shape, jnp.float32),
        in_specs=[SMEM] + [HBM] * len(flat) + [ANY],
        out_specs=VMEM,
        scratch_shapes=[pltpu.VMEM((2,) + shape, jnp.float32), pltpu.SemaphoreType.DMA((2,))],
        compiler_params=pltpu.CompilerParams(vmem_limit_bytes=VMEM_LIMIT),
        cost_estimate=COST,
        name="pass",
    )(turn, *flat, later)


def finish_kernel(counts, place_ref, base_ref, vir_ref, occ_ref, *refs):
    pieces, refs = refs[: sum(counts)], refs[sum(counts) :]
    residual_ref, update_ref, held, sem = refs
    core, y, turn = place_ref[0], place_ref[1], place_ref[2]
    start = 0
    for s, count in enumerate(counts):

        @pl.when(turn == s)
        def _(start=start, count=count):
            copies = [pltpu.make_async_copy(pieces[start + k], held.at[k], sem.at[k]) for k in range(count)]
            for copy in copies:
                copy.start()
            for copy in copies:
                copy.wait()
            for k in range(count, 4):
                held[k] = jnp.zeros(held.shape[1:], jnp.float32)

        start += count
    for half in range(2):
        for which in range(2):
            block = y if which == 0 else 1 - y
            tile = core if half == 0 else 1 - core
            rows = pl.ds(pl.multiple_of(block * 2 * TILE + tile * TILE, TILE), TILE)
            part = pl.ds(which * TILE, TILE)
            ladder = held[2 * half, part] + held[2 * half + 1, part]
            residual = base_ref[rows] + ladder
            residual_ref[rows] = residual
            update_ref[rows] = residual / (vir_ref[rows] + occ_ref[...])


def finish(place, base, vir, occ, pieces):
    shape = jax.ShapeDtypeStruct(base.shape, jnp.float32)
    flat = [piece for stage_pieces in pieces for piece in stage_pieces]
    return pl.pallas_call(
        functools.partial(finish_kernel, tuple(len(p) for p in pieces)),
        out_shape=[shape, shape],
        in_specs=[SMEM, VMEM, VMEM, VMEM] + [HBM] * len(flat),
        out_specs=[VMEM, VMEM],
        scratch_shapes=[
            pltpu.VMEM((4,) + flat[0].shape, jnp.float32),
            pltpu.SemaphoreType.DMA((4,)),
        ],
        compiler_params=pltpu.CompilerParams(vmem_limit_bytes=VMEM_LIMIT),
        cost_estimate=COST,
        name="finish",
    )(place, base, vir, occ, *flat)


def planned(amplitudes, integrals, screen_mask, base_residual, vir_energy, occ_energy):
    both = ("row", "loop")
    zs = range(4)
    row, loop = lax.axis_index("row"), lax.axis_index("loop")
    core, z, y = row % 2, loop // 2, loop % 2
    mask = screen_mask

    def around(x, steps=1):
        return lax.ppermute(x, "loop", [(2 * a + b, 2 * ((a + steps) % 4) + b) for a in zs for b in range(2)])

    def across(x):
        return lax.ppermute(x, "loop", [(a, a ^ 1) for a in range(8)])

    def cores(x):
        return lax.ppermute(x, "row", [(0, 1), (1, 0), (2, 3), (3, 2)])

    def chips(x):
        return lax.ppermute(x, "row", [(0, 2), (2, 0), (1, 3), (3, 1)])

    def to_owner(x, s, flip):
        pairs = [
            ((((a - s) % 4) ^ flip) * 8 + 2 * a + b, ((a - s) % 4) * 8 + 2 * a + b) for a in zs for b in range(2)
        ]
        return lax.ppermute(x, both, pairs)

    def to_chip(x, s):
        pairs = [
            ((((a - s) % 4) ^ c ^ 2) * 8 + 2 * a + b, (((a - s) % 4) ^ c) * 8 + 2 * a + b)
            for a in zs
            for b in range(2)
            for c in range(2)
        ]
        return lax.ppermute(x, both, pairs)

    def place_of(s):
        pair = 2 * ((z - s) % 4)
        return jnp.stack([pair + y, pair + 1 - y, core]).astype(jnp.int32)

    def after(x, *others):
        return lax.optimization_barrier((x, *others))[0]

    def partial(s, cost, mine, other, rests, *earlier):
        return stage(places[s], mask, high, low, mine, other, rests, cost, earlier)

    head, most, last = pack(place_of(0), mask, integrals)
    first_need = needs(after(mask, last))
    need = jnp.maximum(first_need, cores(first_need))
    need = jnp.maximum(need, chips(need)).astype(jnp.int32)
    more, units = need[0, 0], need[1, 0]

    head1 = around(head)
    other_most = across(most)
    zero = jnp.zeros((1,), jnp.int32)
    head2 = around(head1)
    crossed1 = across(head1)
    mixed = rest(place_of(0), zero, mask, [most], [other_most], GROUP, head1)
    rest1 = around(mixed)

    spare = room([last.shape] + [(2 * mask.shape[0] - GROUP, TILE, TILE)] * 3)

    def send_last(carry):
        done, tiles = lax.optimization_barrier((carry[0], last))
        return done + 1, across(tiles)

    more = after(more, mixed)
    other_last = lax.while_loop(lambda c: c[0] < more, send_last, (jnp.int32(0), spare[0]))[1]

    def spill(carry):
        unit, held = carry[0], carry[1:]
        first = (GROUP + UNIT * unit)[None]
        tiles = rest(place_of(0), first, mask, [most, last], [other_most, other_last], UNIT)
        moved = [around(tiles, s) for s in (1, 2, 3)]
        held = [lax.dynamic_update_slice(h, m, (UNIT * unit, 0, 0)) for h, m in zip(held, moved)]
        return (unit + 1, *held)

    units = after(units, mixed)
    spilled = lax.while_loop(lambda c: c[0] < units, spill, (jnp.int32(0), *spare[1:]))[1:]

    places = [place_of(s) for s in range(4)]
    turn = ((z - (row ^ 1)) % 4).astype(jnp.int32)[None]
    place = jnp.stack([core, y, (z - row) % 4]).astype(jnp.int32)
    vir, occ = vir_energy[:, None], occ_energy[None, :]
    high, low = split_array(after(amplitudes, spilled[0], other_last), *places, turn, place, vir, occ)

    keep0, send0 = partial(0, STAGE_COST, [most, last], [other_most, other_last], [])
    total0 = add(keep0, cores(send0))
    moved0 = to_chip(total0, 0)

    head3 = around(head2)
    crossed2 = across(head2)
    rest2 = around(rest1)
    keep1, send1 = partial(1, STAGE_COST, [head1], [crossed1], [rest1, spilled[0]], head2)
    total1 = add(keep1, cores(after(send1, crossed2, total0)))
    moved1 = to_chip(total1, 1)
    crossed3 = across(head3)
    rest3 = around(rest2)

    keep2, send2 = partial(2, COST, [head2], [crossed2], [rest2, spilled[1]], head3, total1)
    total2 = add(keep2, cores(after(send2, rest3, crossed3, moved0, moved1)))
    moved2 = to_chip(total2, 2)

    keep3, send3 = partial(3, STAGE_COST, [head3], [crossed3], [rest3, spilled[2]], total2)
    total3 = add(keep3, cores(after(send3)))
    pieces = [(total0, moved0), (total1, moved1), (total2, moved2)]
    passed = cores(to_pass(turn, pieces, moved2))
    pieces = [pair + (passed,) for pair in pieces]
    pieces.append((total3, to_owner(total3, 3, 2), to_owner(total3, 3, 3), to_owner(total3, 3, 1)))
    return tuple(finish(place, base_residual, vir, occ, pieces))


def solution(mesh):
    in_specs = (
        P("row", "loop"),
        P("row", "loop"),
        P("row", None),
        P("row", "loop"),
        P("row"),
        P("loop"),
    )
    out_specs = (P("row", "loop"), P("row", "loop"))
    body = planned if (mesh.shape["row"], mesh.shape["loop"]) == (4, 8) else gathered
    return jax.shard_map(body, mesh=mesh, in_specs=in_specs, out_specs=out_specs, check_vma=False)
```

```python
import functools

import jax
import jax.numpy as jnp
from jax import lax
from jax.experimental import pallas as pl
from jax.experimental.pallas import tpu as pltpu
from jax.sharding import PartitionSpec as P

TILE = 128
GROUP = 8
HEAD = 16
VMEM_LIMIT = 16 * 1024 * 1024
UNIT = 4

COST = pl.CostEstimate(flops=1, bytes_accessed=1, transcendentals=0)
STAGE_COST = pl.CostEstimate(flops=40 * 1150 * 10**6, bytes_accessed=1, transcendentals=0)
ANY = pl.BlockSpec(memory_space=pl.ANY)
SMEM = pl.BlockSpec(memory_space=pltpu.SMEM)
VMEM = pl.BlockSpec(memory_space=pltpu.VMEM)
HBM = pl.BlockSpec(memory_space=pltpu.HBM)


def expand_mask(screen_mask, tile):
    rows_t, cols_t = screen_mask.shape
    values = screen_mask.astype(jnp.float32)
    return jnp.broadcast_to(values[:, None, :, None], (rows_t, tile, cols_t, tile)).reshape(
        rows_t * tile, cols_t * tile
    )


def gathered(amplitudes, integrals, screen_mask, base_residual, vir_energy, occ_energy):
    full_mask = expand_mask(screen_mask, TILE)
    assembled = lax.all_gather(integrals, "loop", axis=1, tiled=True)
    partial = lax.dot_general(
        assembled * full_mask,
        amplitudes,
        (((0,), (0,)), ((), ())),
        precision=lax.Precision.HIGHEST,
        preferred_element_type=jnp.float32,
    )
    ladder = lax.psum_scatter(partial, "row", scatter_dimension=0, tiled=True)
    residual = base_residual + ladder
    return residual, residual / (vir_energy[:, None] + occ_energy[None, :])


def kept_in_block(mask_ref, block):
    total = jnp.int32(0)
    for i in range(mask_ref.shape[0]):
        total = total + mask_ref[i, 2 * block] + mask_ref[i, 2 * block + 1]
    return total


def needs_kernel(mask_ref, out_ref):
    def step(pair, carry):
        more, units = carry
        rest = jnp.int32(0)
        for which in range(2):
            count = kept_in_block(mask_ref, 2 * pair + which)
            more = jnp.maximum(more, (count > HEAD + GROUP).astype(jnp.int32))
            rest = rest + jnp.maximum(count - HEAD, 0)
        units = jnp.maximum(units, (jnp.maximum(rest - GROUP, 0) + UNIT - 1) // UNIT)
        return more, units

    more, units = lax.fori_loop(0, mask_ref.shape[1] // 4, step, (jnp.int32(0), jnp.int32(0)))
    row = lax.broadcasted_iota(jnp.int32, out_ref.shape, 0)
    out_ref[...] = jnp.where(row == 0, more, units).astype(jnp.float32)


def needs(mask):
    return pl.pallas_call(
        needs_kernel,
        out_shape=jax.ShapeDtypeStruct((8, 128), jnp.float32),
        in_specs=[SMEM],
        out_specs=VMEM,
        cost_estimate=COST,
        name="needs",
    )(mask)


def pack_kernel(place_ref, mask_ref, integrals_ref, *out_refs):
    block = place_ref[0]
    rank = jnp.int32(0)
    for jj in range(2):

        def step(i, rank, jj=jj):
            kept = mask_ref[i, 2 * block + jj]
            row = pl.ds(pl.multiple_of(i * TILE, TILE), TILE)

            @pl.when(kept == 1)
            def _():
                tile = jnp.swapaxes(integrals_ref[row, pl.ds(jj * TILE, TILE)], 0, 1)
                head_ref, most_ref, last_ref = out_refs
                most = most_ref.shape[0]

                @pl.when(rank < HEAD)
                def _():
                    head_ref[rank] = tile

                @pl.when(rank < most)
                def _():
                    most_ref[rank] = tile

                @pl.when(rank >= most)
                def _():
                    last_ref[rank - most] = tile

            return rank + kept

        rank = lax.fori_loop(0, mask_ref.shape[0], step, rank)


def pack(place, mask, integrals):
    sizes = [HEAD, HEAD + GROUP, 2 * mask.shape[0] - HEAD - GROUP]
    shapes = [jax.ShapeDtypeStruct((size, TILE, TILE), jnp.float32) for size in sizes]
    return pl.pallas_call(
        pack_kernel,
        out_shape=shapes,
        in_specs=[SMEM, SMEM, VMEM],
        out_specs=[VMEM] * len(shapes),
        compiler_params=pltpu.CompilerParams(vmem_limit_bytes=VMEM_LIMIT),
        cost_estimate=COST,
        name="pack",
    )(place, mask, integrals)


def rest_kernel(n_mine, place_ref, first_ref, mask_ref, *refs):
    out_ref, held, sem = refs[-3:]
    first, slots = first_ref[0], out_ref.shape[0]
    start = -first
    blocks = (refs[:n_mine], refs[n_mine : 2 * n_mine])
    copies = []
    for which in range(2):
        to = 0
        for part, ref in enumerate(blocks[which]):
            skip = HEAD if part == 0 else 0
            size = ref.shape[0] - skip
            copy = pltpu.make_async_copy(
                ref.at[pl.ds(skip, size)], held.at[which, pl.ds(to, size)], sem.at[len(copies)]
            )
            copy.start()
            copies.append(copy)
            to += size
    for copy in copies:
        copy.wait()
    for which in range(2):
        count = jnp.maximum(kept_in_block(mask_ref, place_ref[which]) - HEAD, 0)
        for k in range(held.shape[1]):
            to = start + k

            @pl.when((k < count) & (to >= 0) & (to < slots))
            def _(k=k, to=to, which=which):
                out_ref[to] = held[which, k]

        start = start + count


def rest(place, first, mask, mine, other, slots, *earlier):
    size = sum(part.shape[0] for part in mine) - HEAD
    return pl.pallas_call(
        functools.partial(rest_kernel, len(mine)),
        out_shape=jax.ShapeDtypeStruct((slots, TILE, TILE), jnp.float32),
        in_specs=[SMEM] * 3 + [ANY] * (len(mine) + len(other) + len(earlier)),
        out_specs=VMEM,
        scratch_shapes=[
            pltpu.VMEM((2, size, TILE, TILE), jnp.float32),
            pltpu.SemaphoreType.DMA((2 * len(mine),)),
        ],
        compiler_params=pltpu.CompilerParams(vmem_limit_bytes=VMEM_LIMIT),
        cost_estimate=COST,
        name="rest",
    )(place, first, mask, *mine, *other, *earlier)


def room(shapes):
    return pl.pallas_call(
        lambda *refs: None,
        out_shape=[jax.ShapeDtypeStruct(shape, jnp.float32) for shape in shapes],
        out_specs=[ANY] * len(shapes),
        name="room",
    )()


def split(x):
    high = x.astype(jnp.bfloat16)
    return high, (x - high.astype(jnp.float32)).astype(jnp.bfloat16)


def split_kernel(x_ref, *refs):
    high_ref, low_ref, held, sem = refs[-4:]
    parts = held.shape[0]
    size = held.shape[1]
    copies = [
        pltpu.make_async_copy(x_ref.at[pl.ds(k * size, size)], held.at[k], sem.at[k]) for k in range(parts)
    ]
    for copy in copies:
        copy.start()
    for k in range(parts):
        copies[k].wait()
        rows = pl.ds(k * size, size)
        high_ref[rows], low_ref[rows] = split(held[k])


def split_array(x, *earlier):
    parts = 8
    shape = pltpu.VMEM(x.shape, jnp.bfloat16)
    return pl.pallas_call(
        split_kernel,
        out_shape=[shape, shape],
        in_specs=[ANY] * (1 + len(earlier)),
        out_specs=[VMEM, VMEM],
        scratch_shapes=[
            pltpu.VMEM((parts, x.shape[0] // parts, x.shape[1]), jnp.float32),
            pltpu.SemaphoreType.DMA((parts,)),
        ],
        compiler_params=pltpu.CompilerParams(vmem_limit_bytes=VMEM_LIMIT),
        cost_estimate=COST,
        name="split",
    )(x, *earlier)


def stage_kernel(sizes, place_ref, mask_ref, high_ref, low_ref, *refs):
    n_mine, n_other, n_rest = sizes
    mine_refs, refs = refs[:n_mine], refs[n_mine:]
    other_refs, refs = refs[:n_other], refs[n_other:]
    rest_refs = refs[:n_rest]
    keep_ref, send_ref, held, sem, i_low, i_high, out, out_sem = refs[-8:]
    rows_t = mask_ref.shape[0]
    stride = held.shape[0] // 2
    chunks, depth, width = i_low.shape[0], i_low.shape[2], high_ref.shape[1]
    step = 256
    core = place_ref[2]

    copies = []

    def bring(ref, start):
        copy = pltpu.make_async_copy(ref, held.at[pl.ds(start, ref.shape[0])], sem.at[len(copies)])
        copy.start()
        copies.append(copy)

    for which, block_refs in enumerate((mine_refs, other_refs)):
        start = which * stride
        for ref in block_refs:
            bring(ref, start)
            start += ref.shape[0]
        if n_rest:
            bring(rest_refs[0], start)
    ranks, totals = [], []
    for which in range(2):
        counts = []
        for jj in range(2):
            count = jnp.int32(0)
            for i in range(rows_t):
                count = count + mask_ref[i, 2 * place_ref[which] + jj]
            counts.append(count)
        ranks += [jnp.int32(0), counts[0]]
        totals.append(counts[0] + counts[1])
    extra = jnp.maximum(totals[0] - HEAD, 0) if n_rest else jnp.int32(0)
    for copy in copies:
        copy.wait()
    if n_rest:

        @pl.when(extra + jnp.maximum(totals[1] - HEAD, 0) > GROUP)
        def _():
            spilled = []
            for which in range(2):
                to = held.at[pl.ds(which * stride + HEAD + GROUP, rest_refs[1].shape[0])]
                spilled.append(pltpu.make_async_copy(rest_refs[1], to, sem.at[which]))
            for copy in spilled:
                copy.start()
            for copy in spilled:
                copy.wait()

    def unpack(k, ranks):
        ranks = list(ranks)
        for q in range(4):
            which, jj = q // 2, q % 2
            rows = pl.ds(q * TILE, TILE)
            for part in range(depth // TILE):
                kept = mask_ref[k * (depth // TILE) + part, 2 * place_ref[which] + jj]
                slot = jnp.where(ranks[q] < HEAD, ranks[q], ranks[q] + (extra if which else 0))
                slot = which * stride + jnp.minimum(slot, stride - 1)
                high, low = split(jnp.where(kept == 1, held[slot], 0.0))
                columns = pl.ds(part * TILE, TILE)
                i_high[k, rows, columns] = high
                i_low[k, rows, columns] = low
                ranks[q] = ranks[q] + kept
        return tuple(ranks)

    lax.fori_loop(0, chunks, unpack, tuple(ranks))

    def dot(a, b):
        return jnp.dot(a, b, preferred_element_type=jnp.float32)

    def out_copies(n):
        columns = pl.ds(pl.multiple_of(n * step, step), step)
        return [
            pltpu.make_async_copy(out.at[part, :, columns], ref.at[:, columns], out_sem.at[n, part])
            for part, ref in enumerate((keep_ref, send_ref))
        ]

    def product(n, carry):
        columns = pl.ds(pl.multiple_of(n * step, step), step)
        total = None
        for k in range(chunks):
            high = high_ref[pl.ds(k * depth, depth), columns]
            low = low_ref[pl.ds(k * depth, depth), columns]
            left = jnp.concatenate([i_low[k], i_high[k], i_high[k]], axis=1)
            part = dot(left, jnp.concatenate([high, low, high], axis=0))
            total = part if total is None else total + part
        first = jnp.concatenate([total[:TILE], total[2 * TILE : 3 * TILE]], axis=0)
        second = jnp.concatenate([total[TILE : 2 * TILE], total[3 * TILE :]], axis=0)
        out[0, :, columns] = jnp.where(core == 0, first, second)
        out[1, :, columns] = jnp.where(core == 0, second, first)
        for copy in out_copies(n):
            copy.start()
        return carry

    lax.fori_loop(0, width // step, product, 0)
    for n in range(width // step):
        for copy in out_copies(n):
            copy.wait()


def stage(place, mask, high, low, mine, other, rests, cost, earlier):
    rows, width = high.shape
    depth = 256
    half = pltpu.HBM((2 * TILE, width), jnp.float32)
    tiles = list(mine) + list(other) + list(rests)
    return pl.pallas_call(
        functools.partial(stage_kernel, (len(mine), len(other), len(rests))),
        out_shape=[half, half],
        in_specs=[SMEM, SMEM, VMEM, VMEM] + [HBM] * (len(tiles) + len(earlier)),
        out_specs=[ANY, ANY],
        scratch_shapes=[
            pltpu.VMEM((2 * (HEAD + 2 * mask.shape[0]), TILE, TILE), jnp.float32),
            pltpu.SemaphoreType.DMA((len(tiles) + 1,)),
            pltpu.VMEM((rows // depth, 4 * TILE, depth), jnp.bfloat16),
            pltpu.VMEM((rows // depth, 4 * TILE, depth), jnp.bfloat16),
            pltpu.VMEM((2, 2 * TILE, width), jnp.float32),
            pltpu.SemaphoreType.DMA((width // 256, 2)),
        ],
        compiler_params=pltpu.CompilerParams(vmem_limit_bytes=VMEM_LIMIT),
        cost_estimate=cost,
        name="stage",
    )(place, mask, *(pltpu.with_memory_space_constraint(a, pltpu.VMEM) for a in (high, low)), *tiles, *(pltpu.with_memory_space_constraint(a, pltpu.HBM) for a in earlier))


def met(*arrays):
    return pl.pallas_call(
        lambda *refs: None,
        out_shape=jax.ShapeDtypeStruct((8, 128), jnp.float32),
        in_specs=[ANY] * len(arrays),
        out_specs=ANY,
        name="met",
    )(*arrays)


def add_kernel(a_ref, b_ref, *refs):
    refs[-1][...] = a_ref[...] + b_ref[...]


def add(a, b, *earlier):
    step = a.shape[0] // 2
    spec = pl.BlockSpec((step, a.shape[1]), lambda i: (i, 0))
    return pl.pallas_call(
        add_kernel,
        grid=(a.shape[0] // step,),
        out_shape=pltpu.HBM(a.shape, a.dtype),
        in_specs=[spec, spec] + [ANY] * len(earlier),
        out_specs=spec,
        compiler_params=pltpu.CompilerParams(vmem_limit_bytes=VMEM_LIMIT),
        cost_estimate=COST,
        name="add",
    )(a, b, *earlier)


def pass_kernel(turn_ref, *refs):
    pieces, (out_ref, held, sem) = refs[:-4], refs[-3:]
    for s in range(len(pieces) // 2):

        @pl.when(turn_ref[0] == s)
        def _():
            copies = [pltpu.make_async_copy(pieces[2 * s + k], held.at[k], sem.at[k]) for k in range(2)]
            for copy in copies:
                copy.start()
            for copy in copies:
                copy.wait()
            out_ref[...] = held[0] + held[1]


def to_pass(turn, pieces, later):
    shape = pieces[0][0].shape
    flat = [piece for pair in pieces for piece in pair]
    return pl.pallas_call(
        pass_kernel,
        out_shape=jax.ShapeDtypeStruct(shape, jnp.float32),
        in_specs=[SMEM] + [HBM] * len(flat) + [ANY],
        out_specs=VMEM,
        scratch_shapes=[pltpu.VMEM((2,) + shape, jnp.float32), pltpu.SemaphoreType.DMA((2,))],
        compiler_params=pltpu.CompilerParams(vmem_limit_bytes=VMEM_LIMIT),
        cost_estimate=COST,
        name="pass",
    )(turn, *flat, later)


def finish_kernel(counts, place_ref, base_ref, vir_ref, occ_ref, *refs):
    pieces, refs = refs[: sum(counts)], refs[sum(counts) :]
    residual_ref, update_ref, held, sem = refs
    core, y, turn = place_ref[0], place_ref[1], place_ref[2]
    start = 0
    for s, count in enumerate(counts):

        @pl.when(turn == s)
        def _(start=start, count=count):
            copies = [pltpu.make_async_copy(pieces[start + k], held.at[k], sem.at[k]) for k in range(count)]
            for copy in copies:
                copy.start()
            for copy in copies:
                copy.wait()
            for k in range(count, 4):
                held[k] = jnp.zeros(held.shape[1:], jnp.float32)

        start += count
    for half in range(2):
        for which in range(2):
            block = y if which == 0 else 1 - y
            tile = core if half == 0 else 1 - core
            rows = pl.ds(pl.multiple_of(block * 2 * TILE + tile * TILE, TILE), TILE)
            part = pl.ds(which * TILE, TILE)
            ladder = held[2 * half, part] + held[2 * half + 1, part]
            residual = base_ref[rows] + ladder
            residual_ref[rows] = residual
            update_ref[rows] = residual / (vir_ref[rows] + occ_ref[...])


def finish(place, base, vir, occ, pieces):
    shape = jax.ShapeDtypeStruct(base.shape, jnp.float32)
    flat = [piece for stage_pieces in pieces for piece in stage_pieces]
    return pl.pallas_call(
        functools.partial(finish_kernel, tuple(len(p) for p in pieces)),
        out_shape=[shape, shape],
        in_specs=[SMEM, VMEM, VMEM, VMEM] + [HBM] * len(flat),
        out_specs=[VMEM, VMEM],
        scratch_shapes=[
            pltpu.VMEM((4,) + flat[0].shape, jnp.float32),
            pltpu.SemaphoreType.DMA((4,)),
        ],
        compiler_params=pltpu.CompilerParams(vmem_limit_bytes=VMEM_LIMIT),
        cost_estimate=COST,
        name="finish",
    )(place, base, vir, occ, *flat)


def planned(amplitudes, integrals, screen_mask, base_residual, vir_energy, occ_energy):
    both = ("row", "loop")
    zs = range(4)
    row, loop = lax.axis_index("row"), lax.axis_index("loop")
    core, z, y = row % 2, loop // 2, loop % 2
    mask = screen_mask

    def around(x, steps=1):
        return lax.ppermute(x, "loop", [(2 * a + b, 2 * ((a + steps) % 4) + b) for a in zs for b in range(2)])

    def across(x):
        return lax.ppermute(x, "loop", [(a, a ^ 1) for a in range(8)])

    def cores(x):
        return lax.ppermute(x, "row", [(0, 1), (1, 0), (2, 3), (3, 2)])

    def chips(x):
        return lax.ppermute(x, "row", [(0, 2), (2, 0), (1, 3), (3, 1)])

    def to_owner(x, s, flip):
        pairs = [
            ((((a - s) % 4) ^ flip) * 8 + 2 * a + b, ((a - s) % 4) * 8 + 2 * a + b) for a in zs for b in range(2)
        ]
        return lax.ppermute(x, both, pairs)

    def to_chip(x, s):
        pairs = [
            ((((a - s) % 4) ^ c ^ 2) * 8 + 2 * a + b, (((a - s) % 4) ^ c) * 8 + 2 * a + b)
            for a in zs
            for b in range(2)
            for c in range(2)
        ]
        return lax.ppermute(x, both, pairs)

    def place_of(s):
        pair = 2 * ((z - s) % 4)
        return jnp.stack([pair + y, pair + 1 - y, core]).astype(jnp.int32)

    def after(x, *others):
        return lax.optimization_barrier((x, *others))[0]

    def partial(s, cost, mine, other, rests, *earlier):
        return stage(places[s], mask, high, low, mine, other, rests, cost, earlier)

    head, most, last = pack(place_of(0), mask, integrals)
    first_need = needs(after(mask, last))
    need = jnp.maximum(first_need, cores(first_need))
    need = jnp.maximum(need, chips(need)).astype(jnp.int32)
    more, units = need[0, 0], need[1, 0]

    head1 = around(head)
    other_most = across(most)
    zero = jnp.zeros((1,), jnp.int32)
    head2 = around(head1)
    crossed1 = across(head1)
    mixed = rest(place_of(0), zero, mask, [most], [other_most], GROUP, head1)
    rest1 = around(mixed)

    spare = room([last.shape] + [(2 * mask.shape[0] - GROUP, TILE, TILE)] * 3)

    def send_last(carry):
        done, tiles = lax.optimization_barrier((carry[0], last))
        return done + 1, across(tiles)

    more = after(more, mixed)
    other_last = lax.while_loop(lambda c: c[0] < more, send_last, (jnp.int32(0), spare[0]))[1]

    def spill(carry):
        unit, held = carry[0], carry[1:]
        first = (GROUP + UNIT * unit)[None]
        tiles = rest(place_of(0), first, mask, [most, last], [other_most, other_last], UNIT)
        moved = [around(tiles, s) for s in (1, 2, 3)]
        held = [lax.dynamic_update_slice(h, m, (UNIT * unit, 0, 0)) for h, m in zip(held, moved)]
        return (unit + 1, *held)

    units = after(units, mixed)
    spilled = lax.while_loop(lambda c: c[0] < units, spill, (jnp.int32(0), *spare[1:]))[1:]

    places = [place_of(s) for s in range(4)]
    turn = ((z - (row ^ 1)) % 4).astype(jnp.int32)[None]
    place = jnp.stack([core, y, (z - row) % 4]).astype(jnp.int32)
    vir, occ = vir_energy[:, None], occ_energy[None, :]
    high, low = split_array(after(amplitudes, spilled[0], other_last), *places, turn, place, vir, occ)

    keep0, send0 = partial(0, STAGE_COST, [most, last], [other_most, other_last], [])
    total0 = add(keep0, cores(send0))
    moved0 = to_chip(total0, 0)

    head3 = around(head2)
    crossed2 = across(head2)
    rest2 = around(rest1)
    keep1, send1 = partial(1, STAGE_COST, [head1], [crossed1], [rest1, spilled[0]], head2, total0)
    total1 = add(keep1, cores(after(send1, crossed2, moved0)))
    moved1 = to_chip(total1, 1)
    crossed3 = across(head3)
    rest3 = around(rest2)

    keep2, send2 = partial(2, COST, [head2], [crossed2], [rest2, spilled[1]], head3, total1)
    total2 = add(keep2, cores(after(send2, rest3, crossed3, moved0, moved1)))
    moved2 = to_chip(total2, 2)

    keep3, send3 = partial(3, STAGE_COST, [head3], [crossed3], [rest3, spilled[2]], total2)
    total3 = add(keep3, cores(after(send3)))
    pieces = [(total0, moved0), (total1, moved1), (total2, moved2)]
    passed = cores(to_pass(turn, pieces, moved2))
    pieces = [pair + (passed,) for pair in pieces]
    pieces.append((total3, to_owner(total3, 3, 2), to_owner(total3, 3, 3), to_owner(total3, 3, 1)))
    return tuple(finish(place, base_residual, vir, occ, pieces))


def solution(mesh):
    in_specs = (
        P("row", "loop"),
        P("row", "loop"),
        P("row", None),
        P("row", "loop"),
        P("row"),
        P("loop"),
    )
    out_specs = (P("row", "loop"), P("row", "loop"))
    body = planned if (mesh.shape["row"], mesh.shape["loop"]) == (4, 8) else gathered
    return jax.shard_map(body, mesh=mesh, in_specs=in_specs, out_specs=out_specs, check_vma=False)
```
